32 devices in a mesh: dp: 8 (over z, y), mp: 4 (over x, core).
Axes of the slice: x: 2, y: 2, z: 4, core: 2. Of those that a mesh axis runs over, the one named last changes fastest.
Arguments:
- texts: bfloat16 [128, 35, 768], P('dp'), may hold values from -6 to 6
- query_weight: bfloat16 [768, 768], P('mp'), may hold values from -0.21875 to 0.21875
- patch_key_value: bfloat16 [32, 12, 577, 128], P('dp', 'mp'), may hold values from -300 to 300
- grad_out: bfloat16 [128, 4, 35, 768], P('dp'), may hold values from -6 to 6
- negatives: int32 [128, 3], P('dp'), may hold values from 0 to 31, as said below
Outputs:
- text_grad: bfloat16 [128, 35, 768], P(('dp', 'mp'))
- weight_grad: float32 [768, 768], P('mp')
- key_value_grad: bfloat16 [32, 12, 577, 128], P('dp', 'mp')
The draws below stay inside these ranges and needn't reach their ends.
Inputs may be any that keep to these rules, and one draw needn't show every extreme that they name: Never an image whose index // 4 equals the text's index // 16. Among the negatives of the texts of one index of dp, at most 12 name images of any one index; some pair of indices reaches 12.
All inputs are finite; a program needn't handle non-finite values.
Results may differ from the reference program's by a relative error of at most 0.03.
The reference program's roundings to bfloat16 on the way (of `query`, `probs`, `dscores` and `dquery`) count: a program that leaves them out, or rounds other values in their place, can miss the bound.
Values may be sent and summed in bfloat16 or wider, within the bound.
A program may use at most 192 MiB of HBM per device.

```python
import jax
import jax.numpy as jnp
from jax import lax

D = 768
HEAD_SIZE = 64
HEADS = 12
PATCHES = 577
TEXT_LEN = 35
NEG = 3
CAPS = 4
IMG_DEV = 4
TXT_DEV = 16
SLOTS = 4
CAP = 12
TEXTS = 128
IMAGES = 32
N_DP = 8


def draw_negatives(key, part):
    key = jax.random.fold_in(key, 7)
    k_rank, k_noise, k_first, k_second, k_order = jax.random.split(key, 5)
    owning_devices = N_DP
    width = owning_devices * CAP
    wanted = NEG * TXT_DEV
    image_frequency = jax.random.permutation(k_rank, owning_devices).astype(jnp.int32)
    extra_score = (owning_devices - image_frequency) * 16 + jnp.where(image_frequency == 0, 1 << 20, 0)
    random_perturb = jax.random.randint(k_noise, (owning_devices, owning_devices, CAP), 0, 1024, dtype=jnp.int32)
    match_score = random_perturb + extra_score[None, :, None]
    sender = jnp.arange(owning_devices, dtype=jnp.int32)
    match_score = jnp.where((sender[:, None] == sender[None, :])[:, :, None], -1, match_score)
    match_score = match_score.reshape(owning_devices, width) * width + jnp.arange(width, dtype=jnp.int32)[None, :]
    _, picked = lax.top_k(match_score, wanted)
    owner = picked.astype(jnp.int32) // CAP
    first = jax.random.randint(k_first, (owning_devices, wanted), 0, IMG_DEV, dtype=jnp.int32)
    second = jax.random.randint(k_second, (owning_devices, wanted), 0, IMG_DEV, dtype=jnp.int32)
    image = owner * IMG_DEV + jnp.minimum(first, second)
    order_keys = jax.random.split(k_order, owning_devices)
    orders = jax.vmap(lambda k: jax.random.permutation(k, wanted))(order_keys).astype(jnp.int32)
    image = jnp.take_along_axis(image, orders, axis=1)
    return image.reshape(owning_devices * TXT_DEV, NEG).astype(jnp.int32)


def draw_patch_key_value(key, part):
    key = jax.random.fold_in(key, 3)
    k_base = jax.random.fold_in(key, 0)
    k_values = jax.random.fold_in(key, 4)
    base = jnp.clip(jax.random.normal(k_base, (IMAGES, PATCHES, D), jnp.float32), -6.0, 6.0)
    keys = base.reshape(IMAGES, PATCHES, HEADS, HEAD_SIZE).transpose(0, 2, 1, 3)
    values = jnp.clip(jax.random.normal(k_values, (IMAGES, HEADS, PATCHES, HEAD_SIZE), jnp.float32), -6.0, 6.0)
    return jnp.concatenate([keys, values], axis=-1).astype(jnp.bfloat16)


def level_of(key, shape, shards, low, top_value):
    loudness = 1.0
    for position, shards_of in shards:
        draws = jax.random.uniform(jax.random.fold_in(jax.random.fold_in(key, 6), position), (shards_of,), jnp.float32, low / len(shards), top_value / len(shards))
        loudness = loudness * jnp.repeat(jnp.exp(draws), shape[position] // shards_of).reshape((-1,) + (1,) * (len(shape) - 1 - position))
    return loudness


def noise(own_key, extent, deviation, limit, cuts=(), held_as=jnp.bfloat16):
    level = level_of(own_key, extent, cuts, -0.22, 0.18) if cuts else 1.0
    drawn = jax.random.normal(own_key, extent, jnp.float32) * deviation * level
    return jnp.minimum(jnp.maximum(drawn, -limit), limit).astype(held_as)


def setup_inputs(seed: int = 0) -> dict:
    seeds = jax.random.split(jax.random.key(seed), 6)
    return {
        "texts": noise(seeds[0], (TEXTS, TEXT_LEN, D), 1.0, 6.0, ((0, 8),)),
        "query_weight": noise(seeds[1], (D, D), D ** -0.5, 0.21875, ((0, 4),)),
        "patch_key_value": draw_patch_key_value(jax.random.fold_in(seeds[5], 71), 0),
        "grad_out": noise(seeds[3], (TEXTS, SLOTS, TEXT_LEN, D), 1.0, 6.0, ((0, 8),)),
        "negatives": draw_negatives(jax.random.fold_in(seeds[5], 71), 0),
    }


def pair_grads(query, cotangent, memory):
    scale = HEAD_SIZE ** -0.5
    q4 = query.reshape(query.shape[:-1] + (-1, HEAD_SIZE)).astype(jnp.float32)
    g4 = cotangent.reshape(cotangent.shape[:-1] + (-1, HEAD_SIZE)).astype(jnp.float32)
    mem = memory.astype(jnp.float32)
    k4 = mem[..., :HEAD_SIZE]
    v4 = mem[..., HEAD_SIZE:]
    scores = jnp.einsum('blhd,bhkd->bhlk', q4, k4) * scale
    probs_f = jax.nn.softmax(scores, axis=-1)
    probs = probs_f.astype(jnp.bfloat16).astype(jnp.float32)
    dprobs = jnp.einsum('blhd,bhkd->bhlk', g4, v4)
    center = jnp.sum(probs_f * dprobs, axis=-1, keepdims=True)
    dscores = (probs_f * (dprobs - center) * scale).astype(jnp.bfloat16).astype(jnp.float32)
    pair_dv = jnp.einsum('bhlk,blhd->bhkd', probs, g4)
    pair_dq = jnp.einsum('bhlk,bhkd->blhd', dscores, k4)
    pair_dk = jnp.einsum('bhlk,blhd->bhkd', dscores, q4)
    pair_dq = pair_dq.reshape(pair_dq.shape[:2] + (-1,))
    return pair_dq, jnp.concatenate([pair_dk, pair_dv], axis=-1)


def reference(texts, query_weight, patch_key_value, grad_out, negatives):
    flat_text = texts.reshape(-1, D)
    query = jnp.dot(flat_text, query_weight.T, preferred_element_type=jnp.float32).astype(jnp.bfloat16)
    query = query.reshape(TEXTS, TEXT_LEN, D)
    own = (jnp.arange(TEXTS, dtype=jnp.int32) // CAPS).astype(jnp.int32)
    chosen = jnp.concatenate([own[:, None], negatives.astype(jnp.int32)], axis=1)
    block = TEXTS // N_DP
    query_blocks = query.reshape(N_DP, block, TEXT_LEN, D)
    grad_blocks = grad_out.reshape(N_DP, block, SLOTS, TEXT_LEN, D)
    image_blocks = chosen.reshape(N_DP, block * SLOTS)

    def visit(memory_acc, item):
        query_tile, g_block, ids = item
        q_rep = jnp.repeat(query_tile, SLOTS, axis=0)
        g_flat = g_block.reshape(block * SLOTS, TEXT_LEN, D)
        memory = jnp.take(patch_key_value, ids, axis=0)
        pair_dq, pair_dkv = pair_grads(q_rep, g_flat, memory)
        memory_acc = memory_acc.at[ids].add(pair_dkv)
        dquery = jnp.sum(pair_dq.reshape(block, SLOTS, TEXT_LEN, D), axis=1)
        return memory_acc, dquery

    start = jnp.zeros((IMAGES, HEADS, PATCHES, 2 * HEAD_SIZE), jnp.float32)
    memory_acc, dquery = lax.scan(visit, start, (query_blocks, grad_blocks, image_blocks))
    dquery = dquery.reshape(-1, D).astype(jnp.bfloat16)
    weight_grad = jnp.dot(dquery.T, flat_text, preferred_element_type=jnp.float32)
    text_grad = jnp.dot(dquery, query_weight, preferred_element_type=jnp.float32).astype(jnp.bfloat16)
    return (text_grad.reshape(TEXTS, TEXT_LEN, D), weight_grad, memory_acc.astype(jnp.bfloat16))
```

```python
import functools

import jax
import jax.numpy as jnp
from jax import lax
from jax.experimental import pallas as pl
from jax.experimental.pallas import tpu as pltpu
from jax.sharding import PartitionSpec as P

HEAD_SIZE = 64
NEG = 3
F32 = jnp.float32
BF16 = jnp.bfloat16
NN = (((1,), (0,)), ((), ()))
NT = (((1,), (1,)), ((), ()))
TN = (((0,), (0,)), ((), ()))


def dot(a, b, dims=NN):
    return lax.dot_general(a, b, dims, preferred_element_type=F32)


def attend(h, chunk, mask, hot, km, vm, kmt, dk, dv, images):
    scale = HEAD_SIZE ** (-0.5)
    zero = jnp.zeros((), BF16)
    qm = jnp.where(mask, jnp.concatenate([chunk[:, :HEAD_SIZE]] * images, axis=1), zero)
    gm = jnp.where(mask, jnp.concatenate([chunk[:, HEAD_SIZE:]] * images, axis=1), zero)
    scores = dot(km[h], qm, NT)
    top = jnp.max(scores, axis=0, keepdims=True)
    e = jnp.exp((scores - top) * scale)
    probs = e * (1.0 / jnp.sum(e, axis=0, keepdims=True))
    dprobs = dot(vm[h], gm, NT)
    center = jnp.sum(probs * dprobs, axis=0, keepdims=True)
    ds = (probs * ((dprobs - center) * scale)).astype(BF16)
    dv[h] += dot(probs.astype(BF16), gm)
    dk[h] += dot(ds, qm)
    wide = dot(kmt[h], ds)
    out = hot[0:1, :] * wide[:HEAD_SIZE]
    for i in range(1, images):
        out += hot[i : i + 1, :] * wide[i * HEAD_SIZE : (i + 1) * HEAD_SIZE]
    return out.T


def kernel(
    n, heads, images, captions, length,
    texts, weight, g_own, g_neg, km, vm, kmt, src_col, srcq_col, srcq_row, ids,
    dq_out, kv_out,
    q_s, own_s, send, recv, idrecv, ret, retrecv, dk, dv, dq_s,
    send_sem, recv_sem, id_send, id_recv, ret_send, ret_recv,
):
    me = lax.axis_index("dp")
    tokens = texts.shape[0]
    count = src_col.shape[1]
    wanted = g_neg.shape[0]
    wide = images * HEAD_SIZE

    barrier = pltpu.get_barrier_semaphore()

    def greet(d, c):
        pl.semaphore_signal(
            barrier, inc=1, device_id={"dp": lax.rem(me + d, n)}, device_id_type=pl.DeviceIdType.MESH
        )
        return c

    lax.fori_loop(1, n, greet, 0)

    def chunk_copy(d):
        return pltpu.make_async_remote_copy(
            src_ref=send.at[d], dst_ref=recv.at[d], send_sem=send_sem.at[d], recv_sem=recv_sem.at[d],
            device_id={"dp": lax.rem(me + d, n)}, device_id_type=pl.DeviceIdType.MESH,
        )

    def id_copy(d):
        to = lax.rem(me + d, n)
        return pltpu.make_async_remote_copy(
            src_ref=ids.at[to], dst_ref=idrecv.at[d], send_sem=id_send.at[d], recv_sem=id_recv.at[d],
            device_id={"dp": to}, device_id_type=pl.DeviceIdType.MESH,
        )

    def ret_copy(d):
        return pltpu.make_async_remote_copy(
            src_ref=ret.at[d], dst_ref=retrecv.at[d], send_sem=ret_send.at[d], recv_sem=ret_recv.at[d],
            device_id={"dp": lax.rem(me + n - d, n)}, device_id_type=pl.DeviceIdType.MESH,
        )

    q_s[...] = dot(texts[...], weight[...], NT).astype(BF16)
    pl.semaphore_wait(barrier, n - 1)

    def pack(d, c):
        to = lax.rem(me + d, n)
        hot_g = (src_col[to] == lax.broadcasted_iota(jnp.int32, (count, wanted), 1)).astype(F32).astype(BF16)
        hot_q = (srcq_col[to] == lax.broadcasted_iota(jnp.int32, (count, tokens), 1)).astype(F32).astype(BF16)
        pq = dot(hot_q, q_s[...]).astype(BF16)
        pg = dot(hot_g, g_neg[...]).astype(BF16)
        for h in range(heads):
            cols = slice(h * HEAD_SIZE, (h + 1) * HEAD_SIZE)
            send[d, h] = jnp.concatenate([pq[:, cols], pg[:, cols]], axis=1)
        chunk_copy(d).start()
        id_copy(d).start()
        return c

    lax.fori_loop(1, n, pack, 0)

    dk[...] = jnp.zeros_like(dk)
    dv[...] = jnp.zeros_like(dv)
    qv, gv = q_s[...], g_own[...]
    for h in range(heads):
        cols = slice(h * HEAD_SIZE, (h + 1) * HEAD_SIZE)
        own_s[h] = jnp.concatenate([qv[:, cols], gv[:, cols]], axis=1)

    per_image = captions * length
    own_mask = (
        lax.broadcasted_iota(jnp.int32, (tokens, wide), 0) // per_image
        == lax.broadcasted_iota(jnp.int32, (tokens, wide), 1) // HEAD_SIZE
    )
    own_hot = (
        lax.broadcasted_iota(jnp.int32, (16, tokens), 1) // per_image
        == lax.broadcasted_iota(jnp.int32, (16, tokens), 0)
    ).astype(F32)

    def own_head(h, c):
        dq = attend(h, own_s[h], own_mask, own_hot, km, vm, kmt, dk, dv, images)
        hi = dq.astype(BF16)
        dq_s[h] = jnp.concatenate([dq, jnp.zeros_like(dq)], axis=1)
        return c

    lax.fori_loop(0, heads, own_head, 0)

    spread = (
        lax.broadcasted_iota(jnp.int32, (16, wide), 0)
        == lax.broadcasted_iota(jnp.int32, (16, wide), 1) // HEAD_SIZE
    ).astype(F32).astype(BF16)

    def serve(d, c):
        chunk_copy(d).wait_recv()
        id_copy(d).wait_recv()
        hot = idrecv[d]
        mask = dot(hot, spread, TN) > 0.5
        hot = hot.astype(F32)

        def head(h, c2):
            dq = attend(h, recv[d, h], mask, hot, km, vm, kmt, dk, dv, images)
            hi = dq.astype(BF16)
            lo = (dq - hi.astype(F32)).astype(BF16)
            ret[d, h] = jnp.concatenate([hi, lo], axis=1)
            return c2

        lax.fori_loop(0, heads, head, 0)
        ret_copy(d).start()
        return c

    lax.fori_loop(1, n, serve, 0)

    for h in range(heads):
        for i in range(images):
            cols = slice(i * HEAD_SIZE, (i + 1) * HEAD_SIZE)
            kv_out[i, h] = jnp.concatenate([dk[h, :, cols], dv[h, :, cols]], axis=1).astype(BF16)

    def collect(d, c):
        ret_copy(d).wait_recv()
        row = srcq_row[lax.rem(me + d, n)][0:1, :]
        hot = (row == lax.broadcasted_iota(jnp.int32, (tokens, count), 0)).astype(F32).astype(BF16)

        def head(h, c2):
            dq_s[h] += dot(hot, retrecv[d, h])
            return c2

        lax.fori_loop(0, heads, head, 0)
        return c

    lax.fori_loop(1, n, collect, 0)
    parts = [dq_s[h, :, :HEAD_SIZE] + dq_s[h, :, HEAD_SIZE:] for h in range(heads)]
    dq_out[...] = jnp.concatenate(parts, axis=1).astype(BF16)

    def drain(d, c):
        chunk_copy(d).wait_send()
        id_copy(d).wait_send()
        ret_copy(d).wait_send()
        return c

    lax.fori_loop(1, n, drain, 0)


def per_device(texts, query_weight, patch_key_value, grad_out, negatives):
    n = lax.axis_size("dp")
    texts_here, length, _ = texts.shape
    images, heads, patches, _ = patch_key_value.shape
    captions = texts_here // images
    wanted = NEG * texts_here
    capacity = 2 * max(1, wanted // n)
    width = query_weight.shape[0]
    tokens = texts_here * length
    count = -(-(capacity * length) // 16) * 16
    flat_text = texts.reshape(tokens, -1)
    grad_cols = lax.dynamic_slice_in_dim(grad_out, lax.axis_index("mp") * width, width, 3)
    g_own = grad_cols[:, 0].reshape(tokens, width)
    g_neg = grad_cols[:, 1:].reshape(wanted * length, width)

    flat_neg = negatives.reshape(-1)
    owner = flat_neg // images
    owner_hot = (owner[:, None] == jnp.arange(n, dtype=jnp.int32)[None, :]).astype(jnp.int32)
    earlier = jnp.cumsum(owner_hot, axis=0) - owner_hot
    rank = jnp.sum(earlier * owner_hot, axis=1)
    slot = owner * capacity + rank
    placed = slot[None, :] == jnp.arange(n * capacity, dtype=jnp.int32)[:, None]
    used = jnp.any(placed, axis=1)
    pair = jnp.sum(jnp.where(placed, jnp.arange(wanted, dtype=jnp.int32)[None, :], 0), axis=1)
    image = jnp.sum(jnp.where(placed, (flat_neg % images)[None, :], 0), axis=1)

    def per_token(start):
        rows = start[:, None] + jnp.arange(length, dtype=jnp.int32)[None, :]
        rows = jnp.where(used[:, None], rows, -1).reshape(n, capacity * length)
        return jnp.pad(rows, ((0, 0), (0, count - capacity * length)), constant_values=-1)

    src = per_token(pair * length)
    srcq = per_token((pair // NEG) * length)
    image_rows = jnp.broadcast_to(jnp.where(used, image, -1)[:, None], (n * capacity, length))
    image_rows = jnp.pad(
        image_rows.reshape(n, capacity * length),
        ((0, 0), (0, count - capacity * length)), constant_values=-1,
    )
    ids = (image_rows[:, None, :] == jnp.arange(16, dtype=jnp.int32)[None, :, None]).astype(BF16)
    srcq_row = jnp.broadcast_to(srcq[:, None, :], (n, 8, count))

    wide = images * HEAD_SIZE
    km = patch_key_value[..., :HEAD_SIZE].transpose(1, 2, 0, 3).reshape(heads, patches, wide)
    vm = patch_key_value[..., HEAD_SIZE:].transpose(1, 2, 0, 3).reshape(heads, patches, wide)
    kmt = km.transpose(0, 2, 1)

    vmem = pl.BlockSpec(memory_space=pltpu.VMEM)
    box = (n, heads, count, 2 * HEAD_SIZE)
    dma = pltpu.SemaphoreType.DMA((n,))
    dquery, key_value_grad = pl.pallas_call(
        functools.partial(kernel, n, heads, images, captions, length),
        out_shape=(
            jax.ShapeDtypeStruct((tokens, width), BF16),
            jax.ShapeDtypeStruct(patch_key_value.shape, BF16),
        ),
        in_specs=[vmem] * 11,
        out_specs=(vmem, vmem),
        scratch_shapes=[
            pltpu.VMEM((tokens, width), BF16),
            pltpu.VMEM((heads, tokens, 2 * HEAD_SIZE), BF16),
            pltpu.VMEM(box, BF16),
            pltpu.VMEM(box, BF16),
            pltpu.VMEM((n, 16, count), BF16),
            pltpu.VMEM(box, BF16),
            pltpu.VMEM(box, BF16),
            pltpu.VMEM((heads, patches, wide), F32),
            pltpu.VMEM((heads, patches, wide), F32),
            pltpu.VMEM((heads, tokens, 2 * HEAD_SIZE), F32),
            dma, dma, dma, dma, dma, dma,
        ],
        compiler_params=pltpu.CompilerParams(
            collective_id=0, has_side_effects=True, vmem_limit_bytes=60 * 1024 * 1024
        ),
    )(
        flat_text, query_weight, g_own, g_neg, km, vm, kmt,
        src[:, :, None], srcq[:, :, None], srcq_row, ids,
    )

    weight_local = dot(dquery, flat_text, TN)
    weight_grad = lax.psum(weight_local, "dp")
    text_term = dot(dquery, query_weight)
    text_grad = lax.psum_scatter(
        text_term.reshape(texts_here, length, -1), "mp", scatter_dimension=0, tiled=True
    )
    return (text_grad.astype(BF16), weight_grad, key_value_grad)


def solution(mesh):
    in_specs = (
        P("dp", None, None),
        P("mp", None),
        P("dp", "mp", None, None),
        P("dp", None, None, None),
        P("dp", None),
    )
    out_specs = (P(("dp", "mp"), None, None), P("mp", None), P("dp", "mp", None, None))
    return jax.shard_map(
        per_device, mesh=mesh, in_specs=in_specs, out_specs=out_specs, check_vma=False
    )
```

```python
import functools

import jax
import jax.numpy as jnp
from jax import lax
from jax.experimental import pallas as pl
from jax.experimental.pallas import tpu as pltpu
from jax.sharding import PartitionSpec as P

HEAD_SIZE = 64
NEG = 3
F32 = jnp.float32
BF16 = jnp.bfloat16
NN = (((1,), (0,)), ((), ()))
NT = (((1,), (1,)), ((), ()))
TN = (((0,), (0,)), ((), ()))


def dot(a, b, dims=NN):
    return lax.dot_general(a, b, dims, preferred_element_type=F32)


def attend(h, chunk, mask, hot, km, vm, kmt, dk, dv, images):
    scale = HEAD_SIZE ** (-0.5)
    zero = jnp.zeros((), BF16)
    qm = jnp.where(mask, jnp.concatenate([chunk[:, :HEAD_SIZE]] * images, axis=1), zero)
    gm = jnp.where(mask, jnp.concatenate([chunk[:, HEAD_SIZE:]] * images, axis=1), zero)
    scores = dot(km[h], qm, NT)
    top = jnp.max(scores, axis=0, keepdims=True)
    e = jnp.exp((scores - top) * scale)
    probs = e * (1.0 / jnp.sum(e, axis=0, keepdims=True))
    dprobs = dot(vm[h], gm, NT)
    center = jnp.sum(probs * dprobs, axis=0, keepdims=True)
    ds = (probs * ((dprobs - center) * scale)).astype(BF16)
    dv[h] += dot(probs.astype(BF16), gm)
    dk[h] += dot(ds, qm)
    wide = dot(kmt[h], ds)
    out = hot[0:1, :] * wide[:HEAD_SIZE]
    for i in range(1, images):
        out += hot[i : i + 1, :] * wide[i * HEAD_SIZE : (i + 1) * HEAD_SIZE]
    return out.T


def kernel(
    n, m, heads, images, captions, length,
    texts, weight, grads, kv, rows,
    text_out, weight_out, kv_out,
    q_s, own_s, send, recv, rowrecv, ret, retrecv, km, vm, kmt, pad_s, dk, dv, dq_s, dqf_s,
    dq_send, dq_recv, w_recv, part_s, part_recv, sum_s, sum_recv,
    send_sem, recv_sem, id_send, id_recv, ret_send, ret_recv, part_ss, part_rs, sum_ss, sum_rs,
    w_ss, w_rs, dq_ss, dq_rs,
):
    me, mine = lax.axis_index("dp"), lax.axis_index("mp")
    tokens = texts.shape[0]
    count = send.shape[2]
    total = grads.shape[0]
    wide = images * HEAD_SIZE
    patches = kv.shape[2]
    share = dq_send.shape[1]
    piece = tokens // m
    band = part_recv.shape[1]
    bands = weight.shape[0] // band
    mesh_id = pl.DeviceIdType.MESH

    barrier = pltpu.get_barrier_semaphore()

    def greet_dp(d, c):
        pl.semaphore_signal(
            barrier, inc=1, device_id={"dp": lax.rem(me + d, n)}, device_id_type=mesh_id
        )
        return c

    def greet_mp(d, c):
        pl.semaphore_signal(
            barrier, inc=1, device_id={"mp": lax.rem(mine + d, m)}, device_id_type=mesh_id
        )
        return c

    lax.fori_loop(1, n, greet_dp, 0)
    lax.fori_loop(1, m, greet_mp, 0)

    def dp_copy(src, dst, ss, rs, to):
        return pltpu.make_async_remote_copy(
            src_ref=src, dst_ref=dst, send_sem=ss, recv_sem=rs, device_id={"dp": to}, device_id_type=mesh_id
        )

    def mp_copy(src, dst, ss, rs, to):
        return pltpu.make_async_remote_copy(
            src_ref=src, dst_ref=dst, send_sem=ss, recv_sem=rs, device_id={"mp": to}, device_id_type=mesh_id
        )

    def chunk_copy(d):
        return dp_copy(send.at[d], recv.at[d], send_sem.at[d], recv_sem.at[d], lax.rem(me + d, n))

    def row_copy(d):
        to = lax.rem(me + d, n)
        return dp_copy(rows.at[to], rowrecv.at[d], id_send.at[d], id_recv.at[d], to)

    def ret_copy(d):
        return dp_copy(ret.at[d], retrecv.at[d], ret_send.at[d], ret_recv.at[d], lax.rem(me + n - d, n))

    def part_copy(d):
        to = lax.rem(me + d, n)
        at = pl.ds(pl.multiple_of(lax.rem(to, bands) * band, 8), band)
        return dp_copy(part_s.at[at], part_recv.at[d], part_ss.at[d], part_rs.at[d], to)

    def sum_copy(d):
        return dp_copy(sum_s, sum_recv.at[d], sum_ss.at[d], sum_rs.at[d], lax.rem(me + d, n))

    def w_copy(d):
        return mp_copy(weight, w_recv.at[d], w_ss.at[d], w_rs.at[d], lax.rem(mine + d, m))

    def dq_copy(d):
        to = lax.rem(mine + d, m)
        return mp_copy(dq_send.at[to], dq_recv.at[d], dq_ss.at[d], dq_rs.at[d], to)

    q_s[...] = dot(texts[...], weight[...], NT).astype(BF16)
    pl.semaphore_wait(barrier, n + m - 2)

    def pack(d, c):
        to = lax.rem(me + d, n)
        columns = rows[to].T[:count].astype(jnp.int32)
        hot_g = (columns[:, 0:1] == lax.broadcasted_iota(jnp.int32, (count, total), 1)).astype(F32).astype(BF16)
        hot_q = (columns[:, 1:2] == lax.broadcasted_iota(jnp.int32, (count, tokens), 1)).astype(F32).astype(BF16)
        pq = dot(hot_q, q_s[...]).astype(BF16)
        pg = dot(hot_g, grads[...]).astype(BF16)
        for h in range(heads):
            cols = slice(h * HEAD_SIZE, (h + 1) * HEAD_SIZE)
            send[d, h] = jnp.concatenate([pq[:, cols], pg[:, cols]], axis=1)
        chunk_copy(d).start()
        row_copy(d).start()
        return c

    lax.fori_loop(1, n, pack, 0)

    def send_w(d, c):
        w_copy(d).start()
        return c

    lax.fori_loop(1, m, send_w, 0)

    pad_s[...] = jnp.zeros_like(pad_s)
    for h in range(heads):
        keys = jnp.concatenate([kv[i, h, :, :HEAD_SIZE] for i in range(images)], axis=1)
        km[h] = keys
        vm[h] = jnp.concatenate([kv[i, h, :, HEAD_SIZE:] for i in range(images)], axis=1)
        pad_s[:patches] = keys
        kmt[h] = pad_s[...].T[:, :patches]
    dk[...] = jnp.zeros_like(dk)
    dv[...] = jnp.zeros_like(dv)
    qv, gv = q_s[...], grads[:tokens]
    for h in range(heads):
        cols = slice(h * HEAD_SIZE, (h + 1) * HEAD_SIZE)
        own_s[h] = jnp.concatenate([qv[:, cols], gv[:, cols]], axis=1)

    per_image = captions * length
    own_mask = (
        lax.broadcasted_iota(jnp.int32, (tokens, wide), 0) // per_image
        == lax.broadcasted_iota(jnp.int32, (tokens, wide), 1) // HEAD_SIZE
    )
    own_hot = (
        lax.broadcasted_iota(jnp.int32, (16, tokens), 1) // per_image
        == lax.broadcasted_iota(jnp.int32, (16, tokens), 0)
    ).astype(F32)

    def own_head(h, c):
        dq = attend(h, own_s[h], own_mask, own_hot, km, vm, kmt, dk, dv, images)
        dq_s[h] = jnp.concatenate([dq, jnp.zeros_like(dq)], axis=1)
        return c

    lax.fori_loop(0, heads, own_head, 0)

    spread = (
        lax.broadcasted_iota(jnp.int32, (16, wide), 0)
        == lax.broadcasted_iota(jnp.int32, (16, wide), 1) // HEAD_SIZE
    ).astype(F32).astype(BF16)

    def serve(d, c):
        chunk_copy(d).wait_recv()
        row_copy(d).wait_recv()
        named = rowrecv[d][2:3, :count].astype(jnp.int32)
        hot = (named == lax.broadcasted_iota(jnp.int32, (16, count), 0)).astype(F32)
        mask = dot(hot.astype(BF16), spread, TN) > 0.5

        def head(h, c2):
            dq = attend(h, recv[d, h], mask, hot, km, vm, kmt, dk, dv, images)
            hi = dq.astype(BF16)
            lo = (dq - hi.astype(F32)).astype(BF16)
            ret[d, h] = jnp.concatenate([hi, lo], axis=1)
            return c2

        lax.fori_loop(0, heads, head, 0)
        ret_copy(d).start()
        return c

    lax.fori_loop(1, n, serve, 0)

    def collect(d, c):
        ret_copy(d).wait_recv()
        row = rows[lax.rem(me + d, n)][1:2, :count].astype(jnp.int32)
        hot = (row == lax.broadcasted_iota(jnp.int32, (tokens, count), 0)).astype(F32).astype(BF16)

        def head(h, c2):
            dq_s[h] += dot(hot, retrecv[d, h])
            return c2

        lax.fori_loop(0, heads, head, 0)
        return c

    lax.fori_loop(1, n, collect, 0)
    parts = [dq_s[h, :, :HEAD_SIZE] + dq_s[h, :, HEAD_SIZE:] for h in range(heads)]
    dqf_s[...] = jnp.concatenate(parts, axis=1)
    dq_send[...] = jnp.zeros_like(dq_send)
    for j in range(m):
        dq_send[j, :piece] = dqf_s[j * piece : (j + 1) * piece].astype(BF16)

    def send_dq(d, c):
        dq_copy(d).start()
        return c

    lax.fori_loop(1, m, send_dq, 0)
    part_s[...] = dot(dqf_s[...].astype(BF16), texts[...], TN)

    def if_band(who, f):
        if bands == n:
            f()
        else:
            pl.when(who < bands)(f)

    def send_part(d, c):
        if_band(lax.rem(me + d, n), lambda: part_copy(d).start())
        return c

    lax.fori_loop(1, n, send_part, 0)

    for h in range(heads):
        for i in range(images):
            cols = slice(i * HEAD_SIZE, (i + 1) * HEAD_SIZE)
            kv_out[i, h] = jnp.concatenate([dk[h, :, cols], dv[h, :, cols]], axis=1).astype(BF16)

    term = dot(dq_send[mine], weight[...])
    for d in range(1, m):
        w_copy(d).wait_recv()
        dq_copy(d).wait_recv()
        term += dot(dq_recv[d], w_recv[d])
    text_out[...] = term.astype(BF16)

    at_mine = pl.ds(pl.multiple_of(lax.rem(me, bands) * band, 8), band)

    def reduce_band():
        sum_s[...] = part_s[at_mine]

        def add(d, c):
            part_copy(d).wait_recv()
            sum_s[...] += part_recv[d]
            return c

        lax.fori_loop(1, n, add, 0)

        def send_sum(d, c):
            sum_copy(d).start()
            return c

        lax.fori_loop(1, n, send_sum, 0)
        weight_out[at_mine] = sum_s[...]

    if_band(me, reduce_band)

    def place(d, c):
        frm = lax.rem(me + n - d, n)

        def put():
            sum_copy(d).wait_recv()
            weight_out[pl.ds(pl.multiple_of(frm * band, 8), band)] = sum_recv[d]

        if_band(frm, put)
        return c

    lax.fori_loop(1, n, place, 0)

    def drain(d, c):
        chunk_copy(d).wait_send()
        row_copy(d).wait_send()
        ret_copy(d).wait_send()
        if_band(lax.rem(me + d, n), lambda: part_copy(d).wait_send())
        if_band(me, lambda: sum_copy(d).wait_send())
        return c

    lax.fori_loop(1, n, drain, 0)

    def drain_mp(d, c):
        w_copy(d).wait_send()
        dq_copy(d).wait_send()
        return c

    lax.fori_loop(1, m, drain_mp, 0)


def per_device(texts, query_weight, patch_key_value, grad_out, negatives):
    n, m = lax.axis_size("dp"), lax.axis_size("mp")
    texts_here, length, _ = texts.shape
    images, heads, patches, _ = patch_key_value.shape
    captions = texts_here // images
    wanted = NEG * texts_here
    capacity = 2 * max(1, wanted // n)
    width, features = query_weight.shape
    tokens = texts_here * length
    count = -(-(capacity * length) // 16) * 16
    lanes = -(-count // 128) * 128
    share = -(-(tokens // m) // 16) * 16
    band = max(8, width // n)
    flat_text = texts.reshape(tokens, -1)
    grad_cols = lax.dynamic_slice_in_dim(grad_out, lax.axis_index("mp") * width, width, 3)
    grads = grad_cols.transpose(1, 0, 2, 3).reshape((NEG + 1) * tokens, width)

    flat_neg = negatives.reshape(-1)
    owner = flat_neg // images
    order = jnp.arange(wanted, dtype=jnp.int32)
    earlier = (owner[:, None] == owner[None, :]) & (order[None, :] < order[:, None])
    slot = owner * capacity + jnp.sum(earlier.astype(jnp.int32), axis=1)
    token = jnp.arange(lanes, dtype=jnp.int32)
    at = jnp.where(token < capacity * length, token // length, -n * capacity)
    place = jnp.arange(n, dtype=jnp.int32)[:, None] * capacity + at[None, :]
    found = place[:, :, None] == slot[None, None, :]
    text = order // NEG
    first = (order % NEG + 1) * tokens + text * length
    facts = jnp.stack([first, text * length, flat_neg % images], axis=0) + 1
    rows = jnp.sum(jnp.where(found[:, None], facts[None, :, None, :], 0), axis=3)
    inside = jnp.stack([token % length, token % length, jnp.zeros_like(token)], axis=0)
    rows = jnp.where(rows > 0, rows - 1 + inside[None], -1)
    rows = jnp.pad(rows, ((0, 0), (0, 5), (0, 0))).astype(F32)

    vmem = pl.BlockSpec(memory_space=pltpu.VMEM)
    box = (n, heads, count, 2 * HEAD_SIZE)
    wide = images * HEAD_SIZE
    dma = pltpu.SemaphoreType.DMA((n,))
    dma_mp = pltpu.SemaphoreType.DMA((m,))
    text_grad, weight_grad, key_value_grad = pl.pallas_call(
        functools.partial(kernel, n, m, heads, images, captions, length),
        out_shape=(
            jax.ShapeDtypeStruct((share, features), BF16),
            jax.ShapeDtypeStruct((width, features), F32),
            jax.ShapeDtypeStruct(patch_key_value.shape, BF16),
        ),
        in_specs=[vmem] * 5,
        out_specs=(vmem, vmem, vmem),
        scratch_shapes=[
            pltpu.VMEM((tokens, width), BF16),
            pltpu.VMEM((heads, tokens, 2 * HEAD_SIZE), BF16),
            pltpu.VMEM(box, BF16),
            pltpu.VMEM(box, BF16),
            pltpu.VMEM((n, 8, lanes), F32),
            pltpu.VMEM(box, BF16),
            pltpu.VMEM(box, BF16),
            pltpu.VMEM((heads, patches, wide), BF16),
            pltpu.VMEM((heads, patches, wide), BF16),
            pltpu.VMEM((heads, wide, patches), BF16),
            pltpu.VMEM((-(-patches // 128) * 128, wide), BF16),
            pltpu.VMEM((heads, patches, wide), F32),
            pltpu.VMEM((heads, patches, wide), F32),
            pltpu.VMEM((heads, tokens, 2 * HEAD_SIZE), F32),
            pltpu.VMEM((tokens, width), F32),
            pltpu.VMEM((m, share, width), BF16),
            pltpu.VMEM((m, share, width), BF16),
            pltpu.VMEM((m, width, features), BF16),
            pltpu.VMEM((width, features), F32),
            pltpu.VMEM((n, band, features), F32),
            pltpu.VMEM((band, features), F32),
            pltpu.VMEM((n, band, features), F32),
            dma, dma, dma, dma, dma, dma, dma, dma, dma, dma,
            dma_mp, dma_mp, dma_mp, dma_mp,
        ],
        compiler_params=pltpu.CompilerParams(
            collective_id=0, has_side_effects=True, vmem_limit_bytes=60 * 1024 * 1024
        ),
    )(flat_text, query_weight, grads, patch_key_value, rows)
    text_grad = text_grad[: tokens // m].reshape(texts_here // m, length, features)
    return (text_grad, weight_grad, key_value_grad)


def solution(mesh):
    in_specs = (
        P("dp", None, None),
        P("mp", None),
        P("dp", "mp", None, None),
        P("dp", None, None, None),
        P("dp", None),
    )
    out_specs = (P(("dp", "mp"), None, None), P("mp", None), P("dp", "mp", None, None))
    return jax.shard_map(
        per_device, mesh=mesh, in_specs=in_specs, out_specs=out_specs, check_vma=False
    )
```

```python
import functools

import jax
import jax.numpy as jnp
from jax import lax
from jax.experimental import pallas as pl
from jax.experimental.pallas import tpu as pltpu
from jax.sharding import PartitionSpec as P

HEAD_SIZE = 64
NEG = 3
F32 = jnp.float32
BF16 = jnp.bfloat16
LOG2E = 1.4426950408889634
NN = (((1,), (0,)), ((), ()))
NT = (((1,), (1,)), ((), ()))
TN = (((0,), (0,)), ((), ()))


def dot(a, b, dims=NN):
    return lax.dot_general(a, b, dims, preferred_element_type=F32)


def attend(h, chunk, mask, hot, km, vm, kmt, dk, dv, images):
    scale = HEAD_SIZE ** (-0.5)
    zero = jnp.zeros((), BF16)
    qm = jnp.where(mask, jnp.concatenate([chunk[:, :HEAD_SIZE]] * images, axis=1), zero)
    gm = jnp.where(mask, jnp.concatenate([chunk[:, HEAD_SIZE:]] * images, axis=1), zero)
    scores = dot(km[h], qm, NT)
    top = jnp.max(scores, axis=0, keepdims=True)
    e = jnp.exp2((scores - top) * (scale * LOG2E))
    probs = e * (1.0 / jnp.sum(e, axis=0, keepdims=True))
    dprobs = dot(vm[h], gm, NT)
    center = jnp.sum(probs * dprobs, axis=0, keepdims=True)
    ds = (probs * (dprobs - center)).astype(BF16)
    dv[h] += dot(probs.astype(BF16), gm)
    dk[h] += dot(ds, qm)
    wide = dot(kmt[h], ds)
    out = hot[0:1, :] * wide[:HEAD_SIZE]
    for i in range(1, images):
        out += hot[i : i + 1, :] * wide[i * HEAD_SIZE : (i + 1) * HEAD_SIZE]
    return out.T


def kernel(
    n, m, heads, images, captions, length,
    texts, weight, grads, kv, rows,
    text_out, weight_out, kv_out,
    q_s, own_s, send, recv, rowrecv, ret, retrecv, km, vm, kmt, pad_s, dk, dv, dq_s, dqf_s,
    dq_send, dq_recv, w_recv, part_s, part_recv, sum_s, sum_recv,
    send_sem, recv_sem, id_send, id_recv, ret_send, ret_recv, part_ss, part_rs, sum_ss, sum_rs,
    w_ss, w_rs, dq_ss, dq_rs,
):
    me, mine = lax.axis_index("dp"), lax.axis_index("mp")
    tokens = texts.shape[0]
    count = send.shape[2]
    total = grads.shape[0]
    wide = images * HEAD_SIZE
    patches = kv.shape[2]
    share = dq_send.shape[1]
    piece = tokens // m
    band = part_recv.shape[1]
    bands = weight.shape[0] // band
    mesh_id = pl.DeviceIdType.MESH

    def peer(j):
        odd = lax.rem(j, 2)
        k = odd * (n // 2) + j // 2
        out = 0
        bit = 1
        while bit < n:
            out = out + lax.rem(me // bit + k // bit, 2) * bit
            bit *= 2
        return out

    barrier = pltpu.get_barrier_semaphore()

    def greet_dp(d, c):
        pl.semaphore_signal(
            barrier, inc=1, device_id={"dp": peer(d)}, device_id_type=mesh_id
        )
        return c

    def greet_mp(d, c):
        pl.semaphore_signal(
            barrier, inc=1, device_id={"mp": lax.rem(mine + d, m)}, device_id_type=mesh_id
        )
        return c

    lax.fori_loop(1, n, greet_dp, 0)
    lax.fori_loop(1, m, greet_mp, 0)

    def dp_copy(src, dst, ss, rs, to):
        return pltpu.make_async_remote_copy(
            src_ref=src, dst_ref=dst, send_sem=ss, recv_sem=rs, device_id={"dp": to}, device_id_type=mesh_id
        )

    def mp_copy(src, dst, ss, rs, to):
        return pltpu.make_async_remote_copy(
            src_ref=src, dst_ref=dst, send_sem=ss, recv_sem=rs, device_id={"mp": to}, device_id_type=mesh_id
        )

    def chunk_copy(d):
        return dp_copy(send.at[d], recv.at[d], send_sem.at[d], recv_sem.at[d], peer(d))

    def row_copy(d):
        to = peer(d)
        return dp_copy(rows.at[to], rowrecv.at[d], id_send.at[d], id_recv.at[d], to)

    def ret_copy(d):
        return dp_copy(ret.at[d], retrecv.at[d], ret_send.at[d], ret_recv.at[d], peer(d))

    def part_copy(d):
        to = peer(d)
        at = pl.ds(pl.multiple_of(lax.rem(to, bands) * band, 8), band)
        return dp_copy(part_s.at[at], part_recv.at[d], part_ss.at[d], part_rs.at[d], to)

    def sum_copy(d):
        return dp_copy(sum_s, sum_recv.at[d], sum_ss.at[d], sum_rs.at[d], peer(d))

    def w_copy(d):
        return mp_copy(weight, w_recv.at[d], w_ss.at[d], w_rs.at[d], lax.rem(mine + d, m))

    def dq_copy(d):
        to = lax.rem(mine + d, m)
        return mp_copy(dq_send.at[to], dq_recv.at[d], dq_ss.at[d], dq_rs.at[d], to)

    q_s[...] = dot(texts[...], weight[...], NT).astype(BF16)
    pl.semaphore_wait(barrier, n + m - 2)

    def pack(d, c):
        to = peer(d)
        columns = rows[to].T[:count].astype(jnp.int32)
        hot_g = (columns[:, 0:1] == lax.broadcasted_iota(jnp.int32, (count, total - tokens), 1) + tokens).astype(F32).astype(BF16)
        hot_q = (columns[:, 1:2] == lax.broadcasted_iota(jnp.int32, (count, tokens), 1)).astype(F32).astype(BF16)
        pq = dot(hot_q, q_s[...]).astype(BF16)
        pg = dot(hot_g, grads[tokens:]).astype(BF16)
        for h in range(heads):
            cols = slice(h * HEAD_SIZE, (h + 1) * HEAD_SIZE)
            send[d, h] = jnp.concatenate([pq[:, cols], pg[:, cols]], axis=1)
        chunk_copy(d).start()
        row_copy(d).start()
        return c

    lax.fori_loop(1, n, pack, 0)

    def send_w(d, c):
        w_copy(d).start()
        return c

    lax.fori_loop(1, m, send_w, 0)

    pad_s[...] = jnp.zeros_like(pad_s)
    for h in range(heads):
        keys = jnp.concatenate([kv[i, h, :, :HEAD_SIZE] for i in range(images)], axis=1)
        km[h] = keys
        values = jnp.concatenate([kv[i, h, :, HEAD_SIZE:] for i in range(images)], axis=1)
        vm[h] = values * jnp.asarray(HEAD_SIZE ** (-0.5), BF16)
        pad_s[:patches] = keys
        kmt[h] = pad_s[...].T[:, :patches]
    dk[...] = jnp.zeros_like(dk)
    dv[...] = jnp.zeros_like(dv)
    qv, gv = q_s[...], grads[:tokens]
    for h in range(heads):
        cols = slice(h * HEAD_SIZE, (h + 1) * HEAD_SIZE)
        own_s[h] = jnp.concatenate([qv[:, cols], gv[:, cols]], axis=1)

    per_image = captions * length
    own_mask = (
        lax.broadcasted_iota(jnp.int32, (tokens, wide), 0) // per_image
        == lax.broadcasted_iota(jnp.int32, (tokens, wide), 1) // HEAD_SIZE
    )
    own_hot = (
        lax.broadcasted_iota(jnp.int32, (16, tokens), 1) // per_image
        == lax.broadcasted_iota(jnp.int32, (16, tokens), 0)
    ).astype(F32)

    def own_head(h, c):
        dq = attend(h, own_s[h], own_mask, own_hot, km, vm, kmt, dk, dv, images)
        dq_s[h] = jnp.concatenate([dq, jnp.zeros_like(dq)], axis=1)
        return c

    lax.fori_loop(0, heads, own_head, 0)

    spread = (
        lax.broadcasted_iota(jnp.int32, (16, wide), 0)
        == lax.broadcasted_iota(jnp.int32, (16, wide), 1) // HEAD_SIZE
    ).astype(F32).astype(BF16)

    late = 3

    def collect(d):
        ret_copy(d).wait_recv()
        row = rows[peer(d)][1:2, :count].astype(jnp.int32)
        hot = (row == lax.broadcasted_iota(jnp.int32, (tokens, count), 0)).astype(F32).astype(BF16)

        def head(h, c2):
            dq_s[h] += dot(hot, retrecv[d, h])
            return c2

        lax.fori_loop(0, heads, head, 0)

    def serve(d, c):
        chunk_copy(d).wait_recv()
        row_copy(d).wait_recv()
        named = rowrecv[d][2:3, :count].astype(jnp.int32)
        hot = (named == lax.broadcasted_iota(jnp.int32, (16, count), 0)).astype(F32)
        mask = dot(hot.astype(BF16), spread, TN) > 0.5

        def head(h, c2):
            dq = attend(h, recv[d, h], mask, hot, km, vm, kmt, dk, dv, images)
            hi = dq.astype(BF16)
            lo = (dq - hi.astype(F32)).astype(BF16)
            ret[d, h] = jnp.concatenate([hi, lo], axis=1)
            return c2

        lax.fori_loop(0, heads, head, 0)
        ret_copy(d).start()

        @pl.when(d > late)
        def _():
            collect(d - late)

        return c

    lax.fori_loop(1, n, serve, 0)
    for d in range(max(1, n - late), n):
        collect(d)
    parts = [dq_s[h, :, :HEAD_SIZE] + dq_s[h, :, HEAD_SIZE:] for h in range(heads)]
    dqf_s[...] = jnp.concatenate(parts, axis=1)
    dq_send[...] = jnp.zeros_like(dq_send)
    for j in range(m):
        dq_send[j, :piece] = dqf_s[j * piece : (j + 1) * piece].astype(BF16)

    def send_dq(d, c):
        dq_copy(d).start()
        return c

    lax.fori_loop(1, m, send_dq, 0)
    part_s[...] = dot(dqf_s[...].astype(BF16), texts[...], TN)

    def if_band(who, f):
        if bands == n:
            f()
        else:
            pl.when(who < bands)(f)

    def send_part(d, c):
        if_band(peer(d), lambda: part_copy(d).start())
        return c

    lax.fori_loop(1, n, send_part, 0)

    for h in range(heads):
        for i in range(images):
            cols = slice(i * HEAD_SIZE, (i + 1) * HEAD_SIZE)
            kv_out[i, h] = jnp.concatenate([dk[h, :, cols], dv[h, :, cols]], axis=1).astype(BF16)

    term = dot(dq_send[mine], weight[...])
    for d in range(1, m):
        w_copy(d).wait_recv()
        dq_copy(d).wait_recv()
        term += dot(dq_recv[d], w_recv[d])
    text_out[...] = term.astype(BF16)

    at_mine = pl.ds(pl.multiple_of(lax.rem(me, bands) * band, 8), band)

    def reduce_band():
        def add(d, c):
            part_copy(d).wait_recv()
            return c + part_recv[d]

        band_sum = lax.fori_loop(1, n, add, part_s[at_mine])
        padding = jnp.zeros((sum_s.shape[0] - band, band_sum.shape[1]), F32)
        sum_s[...] = jnp.concatenate([band_sum, padding], axis=0).astype(BF16)

        def send_sum(d, c):
            sum_copy(d).start()
            return c

        lax.fori_loop(1, n, send_sum, 0)
        weight_out[at_mine] = sum_s[...].astype(F32)[:band]

    if_band(me, reduce_band)

    def place(d, c):
        frm = peer(d)

        def put():
            sum_copy(d).wait_recv()
            weight_out[pl.ds(pl.multiple_of(frm * band, 8), band)] = sum_recv[d].astype(F32)[:band]

        if_band(frm, put)
        return c

    lax.fori_loop(1, n, place, 0)

    def drain(d, c):
        chunk_copy(d).wait_send()
        row_copy(d).wait_send()
        ret_copy(d).wait_send()
        if_band(peer(d), lambda: part_copy(d).wait_send())
        if_band(me, lambda: sum_copy(d).wait_send())
        return c

    lax.fori_loop(1, n, drain, 0)

    def drain_mp(d, c):
        w_copy(d).wait_send()
        dq_copy(d).wait_send()
        return c

    lax.fori_loop(1, m, drain_mp, 0)


def per_device(texts, query_weight, patch_key_value, grad_out, negatives):
    n, m = lax.axis_size("dp"), lax.axis_size("mp")
    texts_here, length, _ = texts.shape
    images, heads, patches, _ = patch_key_value.shape
    captions = texts_here // images
    wanted = NEG * texts_here
    capacity = 2 * max(1, wanted // n)
    width, features = query_weight.shape
    tokens = texts_here * length
    count = -(-(capacity * length) // 16) * 16
    lanes = -(-count // 128) * 128
    share = -(-(tokens // m) // 16) * 16
    band = max(8, width // n)
    flat_text = texts.reshape(tokens, -1)
    grad_cols = lax.dynamic_slice_in_dim(grad_out, lax.axis_index("mp") * width, width, 3)
    grads = grad_cols.transpose(1, 0, 2, 3).reshape((NEG + 1) * tokens, width)

    flat_neg = negatives.reshape(-1)
    owner = flat_neg // images
    order = jnp.arange(wanted, dtype=jnp.int32)
    earlier = (owner[:, None] == owner[None, :]) & (order[None, :] < order[:, None])
    slot = owner * capacity + jnp.sum(earlier.astype(jnp.int32), axis=1)
    token = jnp.arange(lanes, dtype=jnp.int32)
    at = jnp.where(token < capacity * length, token // length, -n * capacity)
    place = jnp.arange(n, dtype=jnp.int32)[:, None] * capacity + at[None, :]
    found = place[:, :, None] == slot[None, None, :]
    text = order // NEG
    first = (order % NEG + 1) * tokens + text * length
    facts = jnp.stack([first, text * length, flat_neg % images], axis=0) + 1
    rows = jnp.sum(jnp.where(found[:, None], facts[None, :, None, :], 0), axis=3)
    inside = jnp.stack([token % length, token % length, jnp.zeros_like(token)], axis=0)
    rows = jnp.where(rows > 0, rows - 1 + inside[None], -1)
    rows = jnp.pad(rows, ((0, 0), (0, 5), (0, 0))).astype(F32)

    vmem = pl.BlockSpec(memory_space=pltpu.VMEM)
    box = (n, heads, count, 2 * HEAD_SIZE)
    wide = images * HEAD_SIZE
    dma = pltpu.SemaphoreType.DMA((n,))
    dma_mp = pltpu.SemaphoreType.DMA((m,))
    text_grad, weight_grad, key_value_grad = pl.pallas_call(
        functools.partial(kernel, n, m, heads, images, captions, length),
        out_shape=(
            jax.ShapeDtypeStruct((share, features), BF16),
            jax.ShapeDtypeStruct((width, features), F32),
            jax.ShapeDtypeStruct(patch_key_value.shape, BF16),
        ),
        in_specs=[vmem] * 5,
        out_specs=(vmem, vmem, vmem),
        scratch_shapes=[
            pltpu.VMEM((tokens, width), BF16),
            pltpu.VMEM((heads, tokens, 2 * HEAD_SIZE), BF16),
            pltpu.VMEM(box, BF16),
            pltpu.VMEM(box, BF16),
            pltpu.VMEM((n, 8, lanes), F32),
            pltpu.VMEM(box, BF16),
            pltpu.VMEM(box, BF16),
            pltpu.VMEM((heads, patches, wide), BF16),
            pltpu.VMEM((heads, patches, wide), BF16),
            pltpu.VMEM((heads, wide, patches), BF16),
            pltpu.VMEM((-(-patches // 128) * 128, wide), BF16),
            pltpu.VMEM((heads, patches, wide), F32),
            pltpu.VMEM((heads, patches, wide), F32),
            pltpu.VMEM((heads, tokens, 2 * HEAD_SIZE), F32),
            pltpu.VMEM((tokens, width), F32),
            pltpu.VMEM((m, share, width), BF16),
            pltpu.VMEM((m, share, width), BF16),
            pltpu.VMEM((m, width, features), BF16),
            pltpu.VMEM((width, features), F32),
            pltpu.VMEM((n, band, features), F32),
            pltpu.VMEM((-(-band // 16) * 16, features), BF16),
            pltpu.VMEM((n, -(-band // 16) * 16, features), BF16),
            dma, dma, dma, dma, dma, dma, dma, dma, dma, dma,
            dma_mp, dma_mp, dma_mp, dma_mp,
        ],
        compiler_params=pltpu.CompilerParams(
            collective_id=0, has_side_effects=True, vmem_limit_bytes=60 * 1024 * 1024
        ),
    )(flat_text, query_weight, grads, patch_key_value, rows)
    text_grad = text_grad[: tokens // m].reshape(texts_here // m, length, features)
    return (text_grad, weight_grad, key_value_grad)


def solution(mesh):
    in_specs = (
        P("dp", None, None),
        P("mp", None),
        P("dp", "mp", None, None),
        P("dp", None, None, None),
        P("dp", None),
    )
    out_specs = (P(("dp", "mp"), None, None), P("mp", None), P("dp", "mp", None, None))
    return jax.shard_map(
        per_device, mesh=mesh, in_specs=in_specs, out_specs=out_specs, check_vma=False
    )
```

```python
import functools

import jax
import jax.numpy as jnp
from jax import lax
from jax.experimental import pallas as pl
from jax.experimental.pallas import tpu as pltpu
from jax.sharding import PartitionSpec as P

HEAD_SIZE = 64
NEG = 3
F32 = jnp.float32
BF16 = jnp.bfloat16
LOG2E = 1.4426950408889634
NN = (((1,), (0,)), ((), ()))
NT = (((1,), (1,)), ((), ()))
TN = (((0,), (0,)), ((), ()))


def dot(a, b, dims=NN):
    return lax.dot_general(a, b, dims, preferred_element_type=F32)


def attend(h, chunk, mask, hot, km, vm, kmt, dk, dv, images):
    scale = HEAD_SIZE ** (-0.5)
    zero = jnp.zeros((), BF16)
    qm = jnp.where(mask, jnp.concatenate([chunk[:, :HEAD_SIZE]] * images, axis=1), zero)
    gm = jnp.where(mask, jnp.concatenate([chunk[:, HEAD_SIZE:]] * images, axis=1), zero)
    scores = dot(km[h], qm, NT)
    top = jnp.max(scores, axis=0, keepdims=True)
    e = jnp.exp2((scores - top) * (scale * LOG2E))
    probs = e * (1.0 / jnp.sum(e, axis=0, keepdims=True))
    dprobs = dot(vm[h], gm, NT)
    center = jnp.sum(probs * dprobs, axis=0, keepdims=True)
    ds = (probs * (dprobs - center)).astype(BF16)
    dv[h] += dot(probs.astype(BF16), gm)
    dk[h] += dot(ds, qm)
    wide = dot(kmt[h], ds)
    out = hot[0:1, :] * wide[:HEAD_SIZE]
    for i in range(1, images):
        out += hot[i : i + 1, :] * wide[i * HEAD_SIZE : (i + 1) * HEAD_SIZE]
    return out.T


def kernel(
    n, m, heads, images, captions, length,
    texts, weight, grads, kv, rows,
    text_out, weight_out, kv_out,
    q_s, own_s, send, recv, rowrecv, ret, retrecv, km, vm, kmt, pad_s, dk, dv, dq_s,
    dq_send, dq_recv, w_recv, part_s, part_recv, sum_s, sum_recv,
    send_sem, recv_sem, id_send, id_recv, ret_send, ret_recv, part_ss, part_rs, sum_ss, sum_rs,
    w_ss, w_rs, dq_ss, dq_rs,
):
    me, mine = lax.axis_index("dp"), lax.axis_index("mp")
    tokens = texts.shape[0]
    count = send.shape[2]
    total = grads.shape[0]
    wide = images * HEAD_SIZE
    patches = kv.shape[2]
    share = dq_send.shape[1]
    piece = tokens // m
    band = part_recv.shape[1]
    bands = weight.shape[0] // band
    mesh_id = pl.DeviceIdType.MESH

    def peer(j):
        odd = lax.rem(j, 2)
        k = odd * (n // 2) + j // 2
        out = 0
        bit = 1
        while bit < n:
            out = out + lax.rem(me // bit + k // bit, 2) * bit
            bit *= 2
        return out

    barrier = pltpu.get_barrier_semaphore()

    def greet_dp(d, c):
        pl.semaphore_signal(
            barrier, inc=1, device_id={"dp": peer(d)}, device_id_type=mesh_id
        )
        return c

    def greet_mp(d, c):
        pl.semaphore_signal(
            barrier, inc=1, device_id={"mp": lax.rem(mine + d, m)}, device_id_type=mesh_id
        )
        return c

    lax.fori_loop(1, n, greet_dp, 0)
    lax.fori_loop(1, m, greet_mp, 0)

    def dp_copy(src, dst, ss, rs, to):
        return pltpu.make_async_remote_copy(
            src_ref=src, dst_ref=dst, send_sem=ss, recv_sem=rs, device_id={"dp": to}, device_id_type=mesh_id
        )

    def mp_copy(src, dst, ss, rs, to):
        return pltpu.make_async_remote_copy(
            src_ref=src, dst_ref=dst, send_sem=ss, recv_sem=rs, device_id={"mp": to}, device_id_type=mesh_id
        )

    def chunk_copy(d):
        return dp_copy(send.at[d], recv.at[d], send_sem.at[d], recv_sem.at[d], peer(d))

    def row_copy(d):
        to = peer(d)
        return dp_copy(rows.at[to], rowrecv.at[d], id_send.at[d], id_recv.at[d], to)

    def ret_copy(d):
        return dp_copy(ret.at[d], retrecv.at[d], ret_send.at[d], ret_recv.at[d], peer(d))

    def part_copy(d):
        to = peer(d)
        at = pl.ds(pl.multiple_of(lax.rem(to, bands) * band, 8), band)
        return dp_copy(part_s.at[at], part_recv.at[d], part_ss.at[d], part_rs.at[d], to)

    def sum_copy(d):
        return dp_copy(sum_s, sum_recv.at[d], sum_ss.at[d], sum_rs.at[d], peer(d))

    def w_copy(d):
        return mp_copy(weight, w_recv.at[d], w_ss.at[d], w_rs.at[d], lax.rem(mine + d, m))

    def dq_copy(d):
        to = lax.rem(mine + d, m)
        return mp_copy(dq_send.at[to], dq_recv.at[d], dq_ss.at[d], dq_rs.at[d], to)

    q_s[...] = dot(texts[...], weight[...], NT).astype(BF16)
    pl.semaphore_wait(barrier, n + m - 2)

    def pack(d, c):
        to = peer(d)
        columns = rows[to].T[:count].astype(jnp.int32)
        hot_g = (columns[:, 0:1] == lax.broadcasted_iota(jnp.int32, (count, total - tokens), 1) + tokens).astype(F32).astype(BF16)
        hot_q = (columns[:, 1:2] == lax.broadcasted_iota(jnp.int32, (count, tokens), 1)).astype(F32).astype(BF16)
        pq = dot(hot_q, q_s[...]).astype(BF16)
        pg = dot(hot_g, grads[tokens:]).astype(BF16)
        for h in range(heads):
            cols = slice(h * HEAD_SIZE, (h + 1) * HEAD_SIZE)
            send[d, h] = jnp.concatenate([pq[:, cols], pg[:, cols]], axis=1)
        chunk_copy(d).start()
        row_copy(d).start()
        return c

    lax.fori_loop(1, n, pack, 0)

    def send_w(d, c):
        w_copy(d).start()
        return c

    lax.fori_loop(1, m, send_w, 0)

    pad_s[...] = jnp.zeros_like(pad_s)
    for h in range(heads):
        keys = jnp.concatenate([kv[i, h, :, :HEAD_SIZE] for i in range(images)], axis=1)
        km[h] = keys
        values = jnp.concatenate([kv[i, h, :, HEAD_SIZE:] for i in range(images)], axis=1)
        vm[h] = values * jnp.asarray(HEAD_SIZE ** (-0.5), BF16)
        pad_s[:patches] = keys
        kmt[h] = pad_s[...].T[:, :patches]
    dk[...] = jnp.zeros_like(dk)
    dv[...] = jnp.zeros_like(dv)
    qv, gv = q_s[...], grads[:tokens]
    for h in range(heads):
        cols = slice(h * HEAD_SIZE, (h + 1) * HEAD_SIZE)
        own_s[h] = jnp.concatenate([qv[:, cols], gv[:, cols]], axis=1)

    held = captions * images
    own_mask = (
        lax.broadcasted_iota(jnp.int32, (tokens, wide), 0) % held // captions
        == lax.broadcasted_iota(jnp.int32, (tokens, wide), 1) // HEAD_SIZE
    )
    own_hot = (
        lax.broadcasted_iota(jnp.int32, (16, tokens), 1) % held // captions
        == lax.broadcasted_iota(jnp.int32, (16, tokens), 0)
    ).astype(F32)

    def own_head(h, c):
        dq = attend(h, own_s[h], own_mask, own_hot, km, vm, kmt, dk, dv, images)
        dq_s[h] = jnp.concatenate([dq, jnp.zeros_like(dq)], axis=1)
        return c

    lax.fori_loop(0, heads, own_head, 0)

    spread = (
        lax.broadcasted_iota(jnp.int32, (16, wide), 0)
        == lax.broadcasted_iota(jnp.int32, (16, wide), 1) // HEAD_SIZE
    ).astype(F32).astype(BF16)

    late = 3

    def collect(d):
        ret_copy(d).wait_recv()
        row = rows[peer(d)][1:2, :count].astype(jnp.int32)
        hot = (row == lax.broadcasted_iota(jnp.int32, (tokens, count), 0)).astype(F32).astype(BF16)

        def head(h, c2):
            dq_s[h] += dot(hot, retrecv[d, h])
            return c2

        lax.fori_loop(0, heads, head, 0)

    def serve(d, c):
        chunk_copy(d).wait_recv()
        row_copy(d).wait_recv()
        named = rowrecv[d][2:3, :count].astype(jnp.int32)
        hot = (named == lax.broadcasted_iota(jnp.int32, (16, count), 0)).astype(F32)
        mask = dot(hot.astype(BF16), spread, TN) > 0.5

        def head(h, c2):
            dq = attend(h, recv[d, h], mask, hot, km, vm, kmt, dk, dv, images)
            hi = dq.astype(BF16)
            lo = (dq - hi.astype(F32)).astype(BF16)
            ret[d, h] = jnp.concatenate([hi, lo], axis=1)
            return c2

        lax.fori_loop(0, heads, head, 0)
        ret_copy(d).start()

        @pl.when(d > late)
        def _():
            collect(d - late)

        return c

    lax.fori_loop(1, n, serve, 0)
    for d in range(max(1, n - late), n):
        collect(d)
    parts = [dq_s[h, :, :HEAD_SIZE] + dq_s[h, :, HEAD_SIZE:] for h in range(heads)]
    dq = jnp.concatenate(parts, axis=1).astype(BF16)
    some = held // m
    row = lax.broadcasted_iota(jnp.int32, (share, tokens), 0)
    row = jnp.where(row < piece, row // some * held + row % some, -held)
    column = lax.broadcasted_iota(jnp.int32, (share, tokens), 1)
    for j in range(m):
        pick = (column == row + j * some).astype(F32).astype(BF16)
        dq_send[j] = dot(pick, dq).astype(BF16)

    def send_dq(d, c):
        dq_copy(d).start()
        return c

    lax.fori_loop(1, m, send_dq, 0)
    part_s[...] = dot(dq, texts[...], TN)

    def if_band(who, f):
        if bands == n:
            f()
        else:
            pl.when(who < bands)(f)

    def send_part(d, c):
        if_band(peer(d), lambda: part_copy(d).start())
        return c

    lax.fori_loop(1, n, send_part, 0)

    for h in range(heads):
        for i in range(images):
            cols = slice(i * HEAD_SIZE, (i + 1) * HEAD_SIZE)
            kv_out[i, h] = jnp.concatenate([dk[h, :, cols], dv[h, :, cols]], axis=1).astype(BF16)

    term = dot(dq_send[mine], weight[...])
    for d in range(1, m):
        w_copy(d).wait_recv()
        dq_copy(d).wait_recv()
        term += dot(dq_recv[d], w_recv[d])
    text_out[...] = term.astype(BF16)

    at_mine = pl.ds(pl.multiple_of(lax.rem(me, bands) * band, 8), band)

    def reduce_band():
        def add(d, c):
            part_copy(d).wait_recv()
            return c + part_recv[d]

        band_sum = lax.fori_loop(1, n, add, part_s[at_mine])
        padding = jnp.zeros((sum_s.shape[0] - band, band_sum.shape[1]), F32)
        sum_s[...] = jnp.concatenate([band_sum, padding], axis=0).astype(BF16)

        def send_sum(d, c):
            sum_copy(d).start()
            return c

        lax.fori_loop(1, n, send_sum, 0)
        weight_out[at_mine] = sum_s[...].astype(F32)[:band]

    if_band(me, reduce_band)

    def place(d, c):
        frm = peer(d)

        def put():
            sum_copy(d).wait_recv()
            weight_out[pl.ds(pl.multiple_of(frm * band, 8), band)] = sum_recv[d].astype(F32)[:band]

        if_band(frm, put)
        return c

    lax.fori_loop(1, n, place, 0)

    def drain(d, c):
        chunk_copy(d).wait_send()
        row_copy(d).wait_send()
        ret_copy(d).wait_send()
        if_band(peer(d), lambda: part_copy(d).wait_send())
        if_band(me, lambda: sum_copy(d).wait_send())
        return c

    lax.fori_loop(1, n, drain, 0)

    def drain_mp(d, c):
        w_copy(d).wait_send()
        dq_copy(d).wait_send()
        return c

    lax.fori_loop(1, m, drain_mp, 0)


def per_device(texts, query_weight, patch_key_value, grad_out, negatives):
    n, m = lax.axis_size("dp"), lax.axis_size("mp")
    texts_here, length, _ = texts.shape
    images, heads, patches, _ = patch_key_value.shape
    captions = texts_here // images
    wanted = NEG * texts_here
    capacity = 2 * max(1, wanted // n)
    width, features = query_weight.shape
    tokens = texts_here * length
    count = -(-(capacity * length) // 16) * 16
    lanes = -(-count // 128) * 128
    share = -(-(tokens // m) // 16) * 16
    band = max(8, width // n)
    flat_text = texts.transpose(1, 0, 2).reshape(tokens, -1)
    grad_cols = lax.dynamic_slice_in_dim(grad_out, lax.axis_index("mp") * width, width, 3)
    grads = grad_cols.transpose(1, 2, 0, 3).reshape((NEG + 1) * tokens, width)

    flat_neg = negatives.reshape(-1)
    owner = flat_neg // images
    order = jnp.arange(wanted, dtype=jnp.int32)
    earlier = (owner[:, None] == owner[None, :]) & (order[None, :] < order[:, None])
    slot = owner * capacity + jnp.sum(earlier.astype(jnp.int32), axis=1)
    token = jnp.arange(lanes, dtype=jnp.int32)
    at = jnp.where(token < capacity * length, token // length, -n * capacity)
    place = jnp.arange(n, dtype=jnp.int32)[:, None] * capacity + at[None, :]
    found = place[:, :, None] == slot[None, None, :]
    text = order // NEG
    first = (order % NEG + 1) * tokens + text
    facts = jnp.stack([first, text, flat_neg % images], axis=0) + 1
    rows = jnp.sum(jnp.where(found[:, None], facts[None, :, None, :], 0), axis=3)
    step = token % length * texts_here
    inside = jnp.stack([step, step, jnp.zeros_like(token)], axis=0)
    rows = jnp.where(rows > 0, rows - 1 + inside[None], -1)
    rows = jnp.pad(rows, ((0, 0), (0, 5), (0, 0))).astype(F32)

    vmem = pl.BlockSpec(memory_space=pltpu.VMEM)
    box = (n, heads, count, 2 * HEAD_SIZE)
    wide = images * HEAD_SIZE
    dma = pltpu.SemaphoreType.DMA((n,))
    dma_mp = pltpu.SemaphoreType.DMA((m,))
    text_grad, weight_grad, key_value_grad = pl.pallas_call(
        functools.partial(kernel, n, m, heads, images, captions, length),
        out_shape=(
            jax.ShapeDtypeStruct((share, features), BF16),
            jax.ShapeDtypeStruct((width, features), F32),
            jax.ShapeDtypeStruct(patch_key_value.shape, BF16),
        ),
        in_specs=[vmem] * 5,
        out_specs=(vmem, vmem, vmem),
        scratch_shapes=[
            pltpu.VMEM((tokens, width), BF16),
            pltpu.VMEM((heads, tokens, 2 * HEAD_SIZE), BF16),
            pltpu.VMEM(box, BF16),
            pltpu.VMEM(box, BF16),
            pltpu.VMEM((n, 8, lanes), F32),
            pltpu.VMEM(box, BF16),
            pltpu.VMEM(box, BF16),
            pltpu.VMEM((heads, patches, wide), BF16),
            pltpu.VMEM((heads, patches, wide), BF16),
            pltpu.VMEM((heads, wide, patches), BF16),
            pltpu.VMEM((-(-patches // 128) * 128, wide), BF16),
            pltpu.VMEM((heads, patches, wide), F32),
            pltpu.VMEM((heads, patches, wide), F32),
            pltpu.VMEM((heads, tokens, 2 * HEAD_SIZE), F32),
            pltpu.VMEM((m, share, width), BF16),
            pltpu.VMEM((m, share, width), BF16),
            pltpu.VMEM((m, width, features), BF16),
            pltpu.VMEM((width, features), F32),
            pltpu.VMEM((n, band, features), F32),
            pltpu.VMEM((-(-band // 16) * 16, features), BF16),
            pltpu.VMEM((n, -(-band // 16) * 16, features), BF16),
            dma, dma, dma, dma, dma, dma, dma, dma, dma, dma,
            dma_mp, dma_mp, dma_mp, dma_mp,
        ],
        compiler_params=pltpu.CompilerParams(
            collective_id=0, has_side_effects=True, vmem_limit_bytes=60 * 1024 * 1024
        ),
    )(flat_text, query_weight, grads, patch_key_value, rows)
    text_grad = text_grad[: tokens // m].reshape(length, texts_here // m, features).transpose(1, 0, 2)
    return (text_grad, weight_grad, key_value_grad)


def solution(mesh):
    in_specs = (
        P("dp", None, None),
        P("mp", None),
        P("dp", "mp", None, None),
        P("dp", None, None, None),
        P("dp", None),
    )
    out_specs = (P(("dp", "mp"), None, None), P("mp", None), P("dp", "mp", None, None))
    return jax.shard_map(
        per_device, mesh=mesh, in_specs=in_specs, out_specs=out_specs, check_vma=False
    )
```

```python
import functools

import jax
import jax.numpy as jnp
from jax import lax
from jax.experimental import pallas as pl
from jax.experimental.pallas import tpu as pltpu
from jax.sharding import PartitionSpec as P

HEAD_SIZE = 64
NEG = 3
F32 = jnp.float32
BF16 = jnp.bfloat16
LOG2E = 1.4426950408889634
NN = (((1,), (0,)), ((), ()))
NT = (((1,), (1,)), ((), ()))
TN = (((0,), (0,)), ((), ()))


def dot(a, b, dims=NN):
    return lax.dot_general(a, b, dims, preferred_element_type=F32)


def attend(h, chunk, mask, hot, km, vm, kmt, dk, dv, images):
    scale = HEAD_SIZE ** (-0.5)
    zero = jnp.zeros((), BF16)
    qm = jnp.where(mask, jnp.concatenate([chunk[:, :HEAD_SIZE]] * images, axis=1), zero)
    gm = jnp.where(mask, jnp.concatenate([chunk[:, HEAD_SIZE:]] * images, axis=1), zero)
    scores = dot(km[h], qm, NT)
    top = jnp.max(scores, axis=0, keepdims=True)
    e = jnp.exp2((scores - top) * (scale * LOG2E))
    probs = e * (1.0 / jnp.sum(e, axis=0, keepdims=True))
    dprobs = dot(vm[h], gm, NT)
    center = jnp.sum(probs * dprobs, axis=0, keepdims=True)
    ds = (probs * (dprobs - center)).astype(BF16)
    dv[h] += dot(probs.astype(BF16), gm)
    dk[h] += dot(ds, qm)
    wide = dot(kmt[h], ds)
    out = hot[0:1, :] * wide[:HEAD_SIZE]
    for i in range(1, images):
        out += hot[i : i + 1, :] * wide[i * HEAD_SIZE : (i + 1) * HEAD_SIZE]
    return out.T


def kernel(
    n, m, heads, images, captions, length,
    texts, weight, grads, kv, rows,
    text_out, weight_out, kv_out,
    q_s, q_all, own_s, chunk_s, send, recv, rowrecv, ret, retrecv, km, vm, kmt, pad_s, dk, dv, dq_s,
    dq_send, dq_recv, w_recv, part_s, part_recv, sum_s, sum_recv,
    send_sem, recv_sem, id_send, id_recv, ret_send, ret_recv, part_ss, part_rs, sum_ss, sum_rs,
    w_ss, w_rs, dq_ss, dq_rs, q_ys, q_zs, q_rs,
):
    me, mine = lax.axis_index("dp"), lax.axis_index("mp")
    tokens = texts.shape[0]
    count = 2 * send.shape[1]
    back = ret.shape[2]
    width = weight.shape[0]
    half = q_all.shape[1]
    floors = n // 2
    floor, side = me // 2, lax.rem(me, 2)
    other = me + 1 - 2 * side
    total = grads.shape[0]
    wide = images * HEAD_SIZE
    patches = kv.shape[2]
    share = dq_send.shape[1]
    piece = tokens // m
    band = part_recv.shape[1]
    bands = weight.shape[0] // band
    mesh_id = pl.DeviceIdType.MESH

    def peer(j):
        odd = lax.rem(j, 2)
        k = odd * (n // 2) + j // 2
        out = 0
        bit = 1
        while bit < n:
            out = out + lax.rem(me // bit + k // bit, 2) * bit
            bit *= 2
        return out

    barrier = pltpu.get_barrier_semaphore()

    def greet_dp(d, c):
        pl.semaphore_signal(
            barrier, inc=1, device_id={"dp": peer(d)}, device_id_type=mesh_id
        )
        return c

    def greet_mp(d, c):
        pl.semaphore_signal(
            barrier, inc=1, device_id={"mp": lax.rem(mine + d, m)}, device_id_type=mesh_id
        )
        return c

    lax.fori_loop(1, n, greet_dp, 0)
    lax.fori_loop(1, m, greet_mp, 0)

    def dp_copy(src, dst, ss, rs, to):
        return pltpu.make_async_remote_copy(
            src_ref=src, dst_ref=dst, send_sem=ss, recv_sem=rs, device_id={"dp": to}, device_id_type=mesh_id
        )

    def mp_copy(src, dst, ss, rs, to):
        return pltpu.make_async_remote_copy(
            src_ref=src, dst_ref=dst, send_sem=ss, recv_sem=rs, device_id={"mp": to}, device_id_type=mesh_id
        )

    def chunk_copy(d):
        return dp_copy(send.at[d], recv.at[d], send_sem.at[d], recv_sem.at[d], peer(d))

    def row_copy(d):
        to = peer(d)
        return dp_copy(rows.at[to], rowrecv.at[d], id_send.at[d], id_recv.at[d], to)

    def ret_copy(d):
        return dp_copy(ret.at[d], retrecv.at[d], ret_send.at[d], ret_recv.at[d], peer(d))

    def part_copy(d):
        to = peer(d)
        at = pl.ds(pl.multiple_of(lax.rem(to, bands) * band, 8), band)
        return dp_copy(part_s.at[at], part_recv.at[d], part_ss.at[d], part_rs.at[d], to)

    def sum_copy(d):
        return dp_copy(sum_s, sum_recv.at[d], sum_ss.at[d], sum_rs.at[d], peer(d))

    def w_copy(d):
        return mp_copy(weight, w_recv.at[d], w_ss.at[d], w_rs.at[d], lax.rem(mine + d, m))

    def dq_copy(d):
        to = lax.rem(mine + d, m)
        return mp_copy(dq_send.at[to], dq_recv.at[d], dq_ss.at[d], dq_rs.at[d], to)

    def q_copy(src, to, ss):
        return dp_copy(q_all.at[src], q_all.at[src], ss, q_rs.at[src], to)

    def pass_on(hop):
        @pl.when(floor - hop >= 0)
        def _():
            src = me - 2 * hop
            q_copy(src, other, q_ys.at[src]).wait_recv()

            @pl.when(floor + 1 < floors)
            def _():
                q_copy(src, me + 2, q_zs.at[src]).start()

            q_copy(src, other, q_ys.at[src]).start()

        @pl.when(floor + hop < floors)
        def _():
            src = me + 2 * hop
            q_copy(src, other, q_ys.at[src]).wait_recv()

            @pl.when(floor > 0)
            def _():
                q_copy(src, me - 2, q_zs.at[src]).start()

            q_copy(src, other, q_ys.at[src]).start()

    query = dot(texts[...], weight[...], NT).astype(BF16)
    q_s[...] = query
    low = jnp.concatenate([query[half:], jnp.zeros((2 * half - tokens, width), BF16)], axis=0)
    q_all[me] = jnp.concatenate([query[:half], low], axis=1)
    pl.semaphore_wait(barrier, n + m - 2)

    @pl.when(floor + 1 < floors)
    def _():
        q_copy(me, me + 2, q_zs.at[me]).start()

    @pl.when(floor > 0)
    def _():
        q_copy(me, me - 2, q_zs.at[n]).start()

    q_copy(me, other, q_ys.at[me]).start()

    def pack(d, c):
        to = peer(d)
        columns = rows[to].T[:count].astype(jnp.int32)
        hot_g = (columns[:, 0:1] == lax.broadcasted_iota(jnp.int32, (count, total - tokens), 1) + tokens).astype(F32).astype(BF16)
        pg = dot(hot_g, grads[tokens:]).astype(BF16)
        send[d] = jnp.concatenate([pg[: count // 2], pg[count // 2 :]], axis=1)
        chunk_copy(d).start()
        row_copy(d).start()
        return c

    lax.fori_loop(1, n, pack, 0)

    def send_w(d, c):
        w_copy(d).start()
        return c

    lax.fori_loop(1, m, send_w, 0)

    pad_s[...] = jnp.zeros_like(pad_s)
    for h in range(heads):
        keys = jnp.concatenate([kv[i, h, :, :HEAD_SIZE] for i in range(images)], axis=1)
        km[h] = keys
        values = jnp.concatenate([kv[i, h, :, HEAD_SIZE:] for i in range(images)], axis=1)
        vm[h] = values * jnp.asarray(HEAD_SIZE ** (-0.5), BF16)
        pad_s[:patches] = keys
        kmt[h] = pad_s[...].T[:, :patches]
    dk[...] = jnp.zeros_like(dk)
    dv[...] = jnp.zeros_like(dv)
    qv, gv = q_s[...], grads[:tokens]
    for h in range(heads):
        cols = slice(h * HEAD_SIZE, (h + 1) * HEAD_SIZE)
        own_s[h] = jnp.concatenate([qv[:, cols], gv[:, cols]], axis=1)

    held = captions * images
    own_mask = (
        lax.broadcasted_iota(jnp.int32, (tokens, wide), 0) % held // captions
        == lax.broadcasted_iota(jnp.int32, (tokens, wide), 1) // HEAD_SIZE
    )
    own_hot = (
        lax.broadcasted_iota(jnp.int32, (16, tokens), 1) % held // captions
        == lax.broadcasted_iota(jnp.int32, (16, tokens), 0)
    ).astype(F32)

    def own_head(h, c):
        dq = attend(h, own_s[h], own_mask, own_hot, km, vm, kmt, dk, dv, images)
        dq_s[h] = jnp.concatenate([dq, jnp.zeros_like(dq)], axis=1)

        @pl.when(h + 1 < floors)
        def _():
            pass_on(h + 1)

        return c

    lax.fori_loop(0, heads, own_head, 0)

    def more(hop, c):
        pass_on(hop)
        return c

    if floors > heads + 1:
        lax.fori_loop(heads + 1, floors, more, 0)

    spread = (
        lax.broadcasted_iota(jnp.int32, (16, wide), 0)
        == lax.broadcasted_iota(jnp.int32, (16, wide), 1) // HEAD_SIZE
    ).astype(F32).astype(BF16)

    late = 3

    def collect(d):
        ret_copy(d).wait_recv()
        row = rows[peer(d)][1:2, :back].astype(jnp.int32)
        hot = (row == lax.broadcasted_iota(jnp.int32, (tokens, back), 0)).astype(F32).astype(BF16)

        def head(h, c2):
            dq_s[h] += dot(hot, retrecv[d, h])
            return c2

        lax.fori_loop(0, heads, head, 0)

    def serve(d, c):
        chunk_copy(d).wait_recv()
        row_copy(d).wait_recv()
        named = rowrecv[d][2:3, :count].astype(jnp.int32)
        hot = (named == lax.broadcasted_iota(jnp.int32, (16, count), 0)).astype(F32)
        mask = dot(hot.astype(BF16), spread, TN) > 0.5
        frm = peer(d)

        @pl.when(lax.rem(frm, 2) != side)
        def _():
            q_copy(frm, other, q_ys.at[frm]).wait_recv()

        column = rowrecv[d].T[:count, 1:2].astype(jnp.int32)
        lane = lax.broadcasted_iota(jnp.int32, (count, half), 1)
        pq = dot((column == lane).astype(F32).astype(BF16), q_all[frm, :, :width])
        pq += dot((column == lane + half).astype(F32).astype(BF16), q_all[frm, :, width:])
        pq = pq.astype(BF16)
        pg = jnp.concatenate([recv[d, :, :width], recv[d, :, width:]], axis=0)
        for h in range(heads):
            cols = slice(h * HEAD_SIZE, (h + 1) * HEAD_SIZE)
            chunk_s[h] = jnp.concatenate([pq[:, cols], pg[:, cols]], axis=1)

        def head(h, c2):
            dq = attend(h, chunk_s[h], mask, hot, km, vm, kmt, dk, dv, images)
            dq = dq[:back]
            hi = dq.astype(BF16)
            lo = (dq - hi.astype(F32)).astype(BF16)
            ret[d, h] = jnp.concatenate([hi, lo], axis=1)
            return c2

        lax.fori_loop(0, heads, head, 0)
        ret_copy(d).start()

        @pl.when(d > late)
        def _():
            collect(d - late)

        return c

    lax.fori_loop(1, n, serve, 0)
    for d in range(max(1, n - late), n):
        collect(d)
    parts = [dq_s[h, :, :HEAD_SIZE] + dq_s[h, :, HEAD_SIZE:] for h in range(heads)]
    dq = jnp.concatenate(parts, axis=1).astype(BF16)
    some = held // m
    row = lax.broadcasted_iota(jnp.int32, (share, tokens), 0)
    row = jnp.where(row < piece, row // some * held + row % some, -held)
    column = lax.broadcasted_iota(jnp.int32, (share, tokens), 1)
    for j in range(m):
        pick = (column == row + j * some).astype(F32).astype(BF16)
        dq_send[j] = dot(pick, dq).astype(BF16)

    def send_dq(d, c):
        dq_copy(d).start()
        return c

    lax.fori_loop(1, m, send_dq, 0)
    part_s[...] = dot(dq, texts[...], TN)

    def if_band(who, f):
        if bands == n:
            f()
        else:
            pl.when(who < bands)(f)

    def send_part(d, c):
        if_band(peer(d), lambda: part_copy(d).start())
        return c

    lax.fori_loop(1, n, send_part, 0)

    for h in range(heads):
        for i in range(images):
            cols = slice(i * HEAD_SIZE, (i + 1) * HEAD_SIZE)
            kv_out[i, h] = jnp.concatenate([dk[h, :, cols], dv[h, :, cols]], axis=1).astype(BF16)

    term = dot(dq_send[mine], weight[...])
    for d in range(1, m):
        w_copy(d).wait_recv()
        dq_copy(d).wait_recv()
        term += dot(dq_recv[d], w_recv[d])
    text_out[...] = term.astype(BF16)

    at_mine = pl.ds(pl.multiple_of(lax.rem(me, bands) * band, 8), band)

    def reduce_band():
        def add(d, c):
            part_copy(d).wait_recv()
            return c + part_recv[d]

        band_sum = lax.fori_loop(1, n, add, part_s[at_mine])
        padding = jnp.zeros((sum_s.shape[0] - band, band_sum.shape[1]), F32)
        sum_s[...] = jnp.concatenate([band_sum, padding], axis=0).astype(BF16)

        def send_sum(d, c):
            sum_copy(d).start()
            return c

        lax.fori_loop(1, n, send_sum, 0)
        weight_out[at_mine] = sum_s[...].astype(F32)[:band]

    if_band(me, reduce_band)

    def place(d, c):
        frm = peer(d)

        def put():
            sum_copy(d).wait_recv()
            weight_out[pl.ds(pl.multiple_of(frm * band, 8), band)] = sum_recv[d].astype(F32)[:band]

        if_band(frm, put)
        return c

    lax.fori_loop(1, n, place, 0)

    def drain(d, c):
        chunk_copy(d).wait_send()
        row_copy(d).wait_send()
        ret_copy(d).wait_send()
        if_band(peer(d), lambda: part_copy(d).wait_send())
        if_band(me, lambda: sum_copy(d).wait_send())
        return c

    lax.fori_loop(1, n, drain, 0)

    def drain_q(z, c):
        src = 2 * z + side
        q_copy(src, other, q_ys.at[src]).wait_send()

        @pl.when((z <= floor) & (floor + 1 < floors))
        def _():
            q_copy(src, other, q_zs.at[src]).wait_send()

        @pl.when((z > floor) & (floor > 0))
        def _():
            q_copy(src, other, q_zs.at[src]).wait_send()

        return c

    lax.fori_loop(0, floors, drain_q, 0)

    @pl.when(floor > 0)
    def _():
        q_copy(me, other, q_zs.at[n]).wait_send()

    def drain_mp(d, c):
        w_copy(d).wait_send()
        dq_copy(d).wait_send()
        return c

    lax.fori_loop(1, m, drain_mp, 0)


def per_device(texts, query_weight, patch_key_value, grad_out, negatives):
    n, m = lax.axis_size("dp"), lax.axis_size("mp")
    texts_here, length, _ = texts.shape
    images, heads, patches, _ = patch_key_value.shape
    captions = texts_here // images
    wanted = NEG * texts_here
    capacity = 2 * max(1, wanted // n)
    width, features = query_weight.shape
    tokens = texts_here * length
    count = -(-(capacity * length) // 32) * 32
    back = -(-(capacity * length) // 16) * 16
    half = -(-tokens // 32) * 16
    lanes = -(-count // 128) * 128
    share = -(-(tokens // m) // 16) * 16
    band = max(8, width // n)
    flat_text = texts.transpose(1, 0, 2).reshape(tokens, -1)
    grad_cols = lax.dynamic_slice_in_dim(grad_out, lax.axis_index("mp") * width, width, 3)
    grads = grad_cols.transpose(1, 2, 0, 3).reshape((NEG + 1) * tokens, width)

    flat_neg = negatives.reshape(-1)
    owner = flat_neg // images
    order = jnp.arange(wanted, dtype=jnp.int32)
    earlier = (owner[:, None] == owner[None, :]) & (order[None, :] < order[:, None])
    slot = owner * capacity + jnp.sum(earlier.astype(jnp.int32), axis=1)
    token = jnp.arange(lanes, dtype=jnp.int32)
    at = jnp.where(token < capacity * length, token // length, -n * capacity)
    place = jnp.arange(n, dtype=jnp.int32)[:, None] * capacity + at[None, :]
    found = place[:, :, None] == slot[None, None, :]
    text = order // NEG
    first = (order % NEG + 1) * tokens + text
    facts = jnp.stack([first, text, flat_neg % images], axis=0) + 1
    rows = jnp.sum(jnp.where(found[:, None], facts[None, :, None, :], 0), axis=3)
    step = token % length * texts_here
    inside = jnp.stack([step, step, jnp.zeros_like(token)], axis=0)
    rows = jnp.where(rows > 0, rows - 1 + inside[None], -1)
    rows = jnp.pad(rows, ((0, 0), (0, 5), (0, 0))).astype(F32)

    vmem = pl.BlockSpec(memory_space=pltpu.VMEM)
    box = (n, heads, back, 2 * HEAD_SIZE)
    grad_box = (n, count // 2, 2 * width)
    wide = images * HEAD_SIZE
    dma = pltpu.SemaphoreType.DMA((n,))
    dma_mp = pltpu.SemaphoreType.DMA((m,))
    text_grad, weight_grad, key_value_grad = pl.pallas_call(
        functools.partial(kernel, n, m, heads, images, captions, length),
        out_shape=(
            jax.ShapeDtypeStruct((share, features), BF16),
            jax.ShapeDtypeStruct((width, features), F32),
            jax.ShapeDtypeStruct(patch_key_value.shape, BF16),
        ),
        in_specs=[vmem] * 5,
        out_specs=(vmem, vmem, vmem),
        scratch_shapes=[
            pltpu.VMEM((tokens, width), BF16),
            pltpu.VMEM((n, half, 2 * width), BF16),
            pltpu.VMEM((heads, tokens, 2 * HEAD_SIZE), BF16),
            pltpu.VMEM((heads, count, 2 * HEAD_SIZE), BF16),
            pltpu.VMEM(grad_box, BF16),
            pltpu.VMEM(grad_box, BF16),
            pltpu.VMEM((n, 8, lanes), F32),
            pltpu.VMEM(box, BF16),
            pltpu.VMEM(box, BF16),
            pltpu.VMEM((heads, patches, wide), BF16),
            pltpu.VMEM((heads, patches, wide), BF16),
            pltpu.VMEM((heads, wide, patches), BF16),
            pltpu.VMEM((-(-patches // 128) * 128, wide), BF16),
            pltpu.VMEM((heads, patches, wide), F32),
            pltpu.VMEM((heads, patches, wide), F32),
            pltpu.VMEM((heads, tokens, 2 * HEAD_SIZE), F32),
            pltpu.VMEM((m, share, width), BF16),
            pltpu.VMEM((m, share, width), BF16),
            pltpu.VMEM((m, width, features), BF16),
            pltpu.VMEM((width, features), F32),
            pltpu.VMEM((n, band, features), F32),
            pltpu.VMEM((-(-band // 16) * 16, features), BF16),
            pltpu.VMEM((n, -(-band // 16) * 16, features), BF16),
            dma, dma, dma, dma, dma, dma, dma, dma, dma, dma,
            dma_mp, dma_mp, dma_mp, dma_mp,
            dma, pltpu.SemaphoreType.DMA((n + 1,)), dma,
        ],
        compiler_params=pltpu.CompilerParams(
            collective_id=0, has_side_effects=True, vmem_limit_bytes=60 * 1024 * 1024
        ),
    )(flat_text, query_weight, grads, patch_key_value, rows)
    text_grad = text_grad[: tokens // m].reshape(length, texts_here // m, features).transpose(1, 0, 2)
    return (text_grad, weight_grad, key_value_grad)


def solution(mesh):
    in_specs = (
        P("dp", None, None),
        P("mp", None),
        P("dp", "mp", None, None),
        P("dp", None, None, None),
        P("dp", None),
    )
    out_specs = (P(("dp", "mp"), None, None), P("mp", None), P("dp", "mp", None, None))
    return jax.shard_map(
        per_device, mesh=mesh, in_specs=in_specs, out_specs=out_specs, check_vma=False
    )
```
